32 devices in a mesh: swath: 2 (over y), shot: 4 (over z), rec: 2 (over x), tr: 2 (over core).
Axes of the slice: x: 2, y: 2, z: 4, core: 2. Of those that a mesh axis runs over, the one named last changes fastest.
Arguments:
- model_init: float32 [8, 512, 2048], P(('swath', 'shot'), None, ('rec', 'tr')), parts along dimension 0, may hold values from -6 to 6
- record: float32 [512, 8192], P(('rec', 'tr'), ('swath', 'shot')), parts along dimension 1, may hold values from -12 to 12
- activation_dither: int32 [8], P(('swath', 'shot')), parts along dimension 0, may hold values from 0 to 511
Outputs:
- model: float32 [8, 512, 2048], P(('swath', 'shot'), None, ('rec', 'tr')), parts along dimension 0
- residual: float32 [512, 8192], P(('rec', 'tr'), ('swath', 'shot')), parts along dimension 1
The draws below stay inside these ranges and needn't reach their ends.
There are 2 independent parts, one for each index of `swath`. The reference program is written for one: setup_inputs(seed, part) draws one part's arguments, and reference() takes and returns one part's arrays. A program takes and returns all parts, laid end to end along the dimension named above; each array names one. Nothing has to cross between parts.
All inputs are finite; a program needn't handle non-finite values.
Results may differ from the reference program's by a relative error of at most 0.012.
The reference program's roundings to bfloat16 on the way count: a program that leaves them out, or rounds other values in their place, can miss the bound.
Values may be sent and summed in bfloat16 or wider, within the bound.
A program may use at most 64 MiB of HBM per device.

```python
import math
import jax
import jax.numpy as jnp
from jax import lax

CLOCK_LEVELS = 2048
R = 512
ITERS = 2
ACTIVATION_GAP = 1024
JIT = 512
WIN = 1024
HOPS = 2
GUN_LINE_EMITTERS = 4
TREC = 4096


def place_ends(drawn, stream_key, low, largest):
    spot = [jax.random.randint(jax.random.fold_in(stream_key, axis), (), 0, length) for axis, length in enumerate(drawn.shape)]
    widest = drawn.shape.index(max(drawn.shape))
    neighbour = spot[:widest] + [(spot[widest] + 1) % drawn.shape[widest]] + spot[widest + 1:]
    return drawn.at[tuple(spot)].set(low).at[tuple(neighbour)].set(largest)


def block_scale(rng, extent, cuts, low, top_value):
    loudness, own = 1.0, jax.random.fold_in(rng, 6)
    for axis_at, blocks in cuts:
        draws = jnp.exp(jax.random.uniform(jax.random.fold_in(own, axis_at), (blocks,), jnp.float32, low / len(cuts), top_value / len(cuts)))
        loudness = loudness * jnp.repeat(draws, extent[axis_at] // blocks).reshape([-1 if axis == axis_at else 1 for axis in range(len(extent))])
    return loudness


def bell_draw(stream_key, dims, scale, limit, cuts=(), kind=jnp.bfloat16):
    entries = scale * jax.random.normal(stream_key, dims, jnp.float32)
    if cuts:
        entries = entries * block_scale(stream_key, dims, cuts, -0.22, 0.18)
    return jnp.clip(entries, -limit, limit).astype(kind)


def setup_inputs(seed: int = 0, part: int = 0) -> dict:
    seeds = jax.random.split(jax.random.key(seed), 4)
    own_keys = jax.random.split(jax.random.fold_in(seeds[3], part), 4)
    model_init = bell_draw(own_keys[0], (GUN_LINE_EMITTERS, R, CLOCK_LEVELS), 1.0, 6.0, ((0, 4), (2, 4)), jnp.float32)
    record = bell_draw(own_keys[1], (R, TREC), 2.0, 12.0, ((0, 4), (1, 4)), jnp.float32)
    activation_dither = place_ends(jax.random.randint(own_keys[2], (GUN_LINE_EMITTERS,), 0, JIT), jax.random.fold_in(own_keys[2], 1), 0, JIT - 1).astype(jnp.int32)
    return {"model_init": model_init, "record": record, "activation_dither": activation_dither}


def cosine_table(order):
    emitter_location = jnp.arange(order, dtype=jnp.int32)
    phase = (2 * emitter_location[None, :] + 1) * emitter_location[:, None] % (4 * order)
    table = jnp.cos(math.pi * phase.astype(jnp.float32) / (2.0 * order)) * math.sqrt(2.0 / order)
    table = table * jnp.where(emitter_location[:, None] == 0, math.sqrt(0.5), 1.0).astype(jnp.float32)
    return table.astype(jnp.bfloat16)

def reference(model_init, record, activation_dither):
    time_table = cosine_table(CLOCK_LEVELS).astype(jnp.float32)
    trace_table = cosine_table(R).astype(jnp.float32)
    padded_epochs = jnp.arange(GUN_LINE_EMITTERS, dtype=jnp.int32) * ACTIVATION_GAP + activation_dither.astype(jnp.int32)
    margin = (HOPS + 1) * WIN
    model = model_init
    residual = record
    for sweep in range(ITERS):
        narrow_model = model.astype(jnp.bfloat16).astype(jnp.float32)
        spread = jnp.einsum('skf,kr->srf', narrow_model, trace_table).astype(jnp.bfloat16)
        shots = jnp.einsum('srf,ft->srt', spread.astype(jnp.float32), time_table)

        def place(emitter_location, buffer):
            activation_delay = padded_epochs[emitter_location]
            current = lax.dynamic_slice_in_dim(buffer, activation_delay, CLOCK_LEVELS, 1)
            return lax.dynamic_update_slice_in_dim(buffer, current + shots[emitter_location], activation_delay, 1)
        buffer = lax.fori_loop(0, GUN_LINE_EMITTERS, place, jnp.zeros((R, JIT + TREC + margin), jnp.float32))
        residual = record - buffer[:, JIT:JIT + TREC]
        bounded_emitter_group = jnp.concatenate([jnp.zeros((R, JIT), jnp.bfloat16), residual.astype(jnp.bfloat16), jnp.zeros((R, margin), jnp.bfloat16)], axis=1)
        emitter_pieces = jax.vmap(lambda activation_delay: lax.dynamic_slice_in_dim(bounded_emitter_group, activation_delay, CLOCK_LEVELS, 1))(padded_epochs)
        spectra = jnp.einsum('srt,ft->srf', emitter_pieces.astype(jnp.float32), time_table).astype(jnp.bfloat16)
        grad = jnp.einsum('srf,kr->skf', spectra.astype(jnp.float32), trace_table)
        value = model + 0.5 * grad
        model = jnp.sign(value) * jnp.maximum(jnp.abs(value) - 0.3, 0.0)
    return (model, residual)
```

```python
import math

import jax
import jax.numpy as jnp
import ml_dtypes
import numpy as np
from jax import lax
from jax.sharding import PartitionSpec as P

ITERS = 2


def passed_along(value, axis, steps):
    count = lax.axis_size(axis)
    first, last = (max(0, -steps), min(count, count - steps))
    return lax.ppermute(value, axis, [(source, source + steps) for source in range(first, last)])


def cosine_table(order):
    column = np.arange(order, dtype=np.int64)
    phase = (2 * column[None, :] + 1) * column[:, None] % (4 * order)
    table = np.cos(np.float32(math.pi) * phase.astype(np.float32) / np.float32(2.0 * order))
    table = table * np.float32(math.sqrt(2.0 / order))
    table = table * np.where(column[:, None] == 0, math.sqrt(0.5), 1.0).astype(np.float32)
    return table.astype(ml_dtypes.bfloat16)


def shards(model_init, record, activation_dither):
    shots_dev, traces, freq_dev = model_init.shape
    traces_dev, window = record.shape
    time_len = freq_dev * lax.axis_size(("rec", "tr"))
    spacing = time_len // 2
    jitter = time_len // 4
    hops = (time_len - 2) // window
    margin = (hops + 1) * window
    time_table = jnp.asarray(cosine_table(time_len))
    trace_table = jnp.asarray(cosine_table(traces))
    starts = jnp.arange(shots_dev, dtype=jnp.int32) * spacing + activation_dither - jitter + window
    width = window + margin
    model = model_init
    residual = record
    for sweep in range(ITERS):
        spread = jnp.einsum(
            "skf,kr->srf",
            model.astype(jnp.bfloat16),
            trace_table,
            preferred_element_type=jnp.float32,
        ).astype(jnp.bfloat16)
        shot_data = jnp.einsum(
            "srf,ft->srt",
            lax.all_to_all(spread, ("rec", "tr"), split_axis=1, concat_axis=2, tiled=True),
            time_table,
            preferred_element_type=jnp.float32,
        )
        buffer = jnp.zeros((traces_dev, width), jnp.float32)
        buffer = lax.dynamic_update_slice_in_dim(buffer, shot_data[0], starts[0], 1)
        predicted = buffer[:, window : 2 * window]
        predicted = predicted + passed_along(buffer[:, :window], "shot", -1)
        for hop in range(1, hops + 1):
            predicted = predicted + passed_along(
                buffer[:, (hop + 1) * window : (hop + 2) * window], "shot", hop
            )
        residual = record - predicted
        narrow = residual.astype(jnp.bfloat16)
        earlier = passed_along(narrow, "shot", 1)
        later = [passed_along(narrow, "shot", -hop) for hop in range(1, hops + 1)]
        padded = jnp.concatenate([earlier, narrow] + later, axis=1)
        emitter_pieces = jnp.stack(
            [lax.dynamic_slice_in_dim(padded, starts[0], time_len, 1)], axis=0
        )
        spectra = jnp.einsum(
            "srt,ft->srf", emitter_pieces, time_table, preferred_element_type=jnp.float32
        ).astype(jnp.bfloat16)
        grad = jnp.einsum(
            "srf,kr->skf",
            lax.all_to_all(spectra, ("rec", "tr"), split_axis=2, concat_axis=1, tiled=True),
            trace_table,
            preferred_element_type=jnp.float32,
        )
        value = model + 0.5 * grad
        model = jnp.sign(value) * jnp.maximum(jnp.abs(value) - 0.3, 0.0)
    return (model, residual)


def solution(mesh):
    return jax.shard_map(
        shards,
        mesh=mesh,
        in_specs=(
            P(("swath", "shot"), None, ("rec", "tr")),
            P(("rec", "tr"), ("swath", "shot")),
            P(("swath", "shot")),
        ),
        out_specs=(P(("swath", "shot"), None, ("rec", "tr")), P(("rec", "tr"), ("swath", "shot"))),
        check_vma=False,
    )
```

```python
import functools
import math

import jax
import jax.numpy as jnp
import ml_dtypes
import numpy as np
from jax import lax
from jax.experimental import pallas as pl
from jax.experimental.pallas import tpu as pltpu
from jax.sharding import PartitionSpec as P

ITERS = 2
CHUNK = 32
TILE = 512
BF = jnp.bfloat16
F32 = jnp.float32


def cosine_table(order):
    column = np.arange(order, dtype=np.int64)
    phase = (2 * column[None, :] + 1) * column[:, None] % (4 * order)
    table = np.cos(np.float32(math.pi) * phase.astype(np.float32) / np.float32(2.0 * order))
    table = table * np.float32(math.sqrt(2.0 / order))
    table = table * np.where(column[:, None] == 0, math.sqrt(0.5), 1.0).astype(np.float32)
    return table.astype(ml_dtypes.bfloat16)


def dot(a, b):
    return jnp.dot(a, b, preferred_element_type=F32)


def kernel(
    sizes, dither, model_in, record, trace_table, trace_table_t, time_hbm, time_t_hbm,
    model, residual,
    time_table, time_table_t, narrow_model, spread_out, spread_in, shot_sum, up_out, down_out,
    up_in, down_in, narrow, tail_in, head_in, windows, spectra_out, spectra_in,
    table_sem, spread_send, spread_recv, part_send, part_recv, res_send, res_recv,
    spectra_send, spectra_recv,
):
    recs, cores, shots, time_len, freqs, traces, window = sizes
    jitter = time_len // 4
    span = time_len + jitter
    high = jitter + window
    rec, core, shot = lax.axis_index("rec"), lax.axis_index("tr"), lax.axis_index("shot")
    me = rec * cores + core
    offsets = [(a, b) for a in range(1, recs) for b in range(cores)]
    offsets += [(0, b) for b in range(1, cores)]
    has_before, has_after = shot > 0, shot < shots - 1

    def peer(a, b):
        return lax.rem(rec + a, recs), lax.rem(core + b, cores)

    def origin(a, b):
        return lax.rem(rec + recs - a, recs), lax.rem(core + cores - b, cores)

    def rows_of(index, size):
        return pl.ds(pl.multiple_of(index * size, size), size)

    copy_a = pltpu.make_async_copy(time_hbm, time_table, table_sem.at[0])
    copy_b = pltpu.make_async_copy(time_t_hbm, time_table_t, table_sem.at[1])
    copy_a.start()
    copy_b.start()

    barrier = pltpu.get_barrier_semaphore()
    for a, b in offsets:
        to_rec, to_core = peer(a, b)
        pl.semaphore_signal(barrier, inc=1, device_id={"rec": to_rec, "tr": to_core})

    @pl.when(has_before)
    def _():
        pl.semaphore_signal(barrier, inc=1, device_id={"shot": shot - 1})

    @pl.when(has_after)
    def _():
        pl.semaphore_signal(barrier, inc=1, device_id={"shot": shot + 1})

    model[...] = model_in[...]
    narrow_model[...] = model_in[...].astype(BF)

    @pl.when(jnp.logical_not(has_before))
    def _():
        tail_in[...] = jnp.zeros_like(tail_in)

    @pl.when(jnp.logical_not(has_after))
    def _():
        head_in[...] = jnp.zeros_like(head_in)

    beside = has_before.astype(jnp.int32) + has_after.astype(jnp.int32)
    pl.semaphore_wait(barrier, len(offsets) + beside)

    delay = dither[0]
    back = jnp.where(delay == 0, 0, span - delay)

    def spread_copy(it, j, slot):
        to_rec, to_core = peer(*offsets[j])
        return pltpu.make_async_remote_copy(
            spread_out.at[it, j], spread_in.at[it, slot], spread_send.at[it, j],
            spread_recv.at[it, j], device_id={"rec": to_rec, "tr": to_core},
        )

    def spectra_copy(it, j, slot):
        to_rec, to_core = peer(*offsets[j])
        return pltpu.make_async_remote_copy(
            spectra_out.at[it, j], spectra_in.at[it, rows_of(slot, traces)],
            spectra_send.at[it, j], spectra_recv.at[it, j],
            device_id={"rec": to_rec, "tr": to_core},
        )

    def up_copy(it, c):
        rows = pl.ds(c * CHUNK, CHUNK)
        return pltpu.make_async_remote_copy(
            up_out.at[it, rows], up_in.at[it, rows], part_send.at[it, 0, c],
            part_recv.at[it, 0, c], device_id={"shot": shot + 1},
        )

    def down_copy(it, c):
        rows = pl.ds(c * CHUNK, CHUNK)
        return pltpu.make_async_remote_copy(
            down_out.at[it, rows], down_in.at[it, rows], part_send.at[it, 1, c],
            part_recv.at[it, 1, c], device_id={"shot": shot - 1},
        )

    def tail_copy(it, c):
        rows = pl.ds(c * CHUNK, CHUNK)
        return pltpu.make_async_remote_copy(
            narrow.at[it, rows, pl.ds(window - jitter, jitter)], tail_in.at[it, rows],
            res_send.at[it, 0, c], res_recv.at[it, 0, c], device_id={"shot": shot + 1},
        )

    def head_copy(it, c):
        rows = pl.ds(c * CHUNK, CHUNK)
        return pltpu.make_async_remote_copy(
            narrow.at[it, rows], head_in.at[it, rows],
            res_send.at[it, 1, c], res_recv.at[it, 1, c], device_id={"shot": shot - 1},
        )

    chunks = traces // CHUNK
    for it in range(ITERS):
        for j, (a, b) in enumerate(offsets):
            to_rec, to_core = peer(a, b)
            block = dot(trace_table_t[rows_of(to_rec * cores + to_core, traces), :], narrow_model[...])
            spread_out[it, j] = block.astype(BF)
            spread_copy(it, j, me).start()
        spread_in[it, me] = dot(trace_table_t[rows_of(me, traces), :], narrow_model[...]).astype(BF)
        if it == 0:
            copy_a.wait()

        def add_block(slot, first):
            @pl.loop(0, time_len // TILE)
            def _(i):
                columns = pl.ds(pl.multiple_of(i * TILE, TILE), TILE)
                term = dot(spread_in[it, slot], time_table[rows_of(slot, freqs), columns])
                if first:
                    shot_sum[:, columns] = term
                else:
                    shot_sum[:, columns] += term

        add_block(me, True)
        for j in list(range(len(offsets)))[::-1][: cores - 1] + list(range(len(offsets)))[: -(cores - 1)]:
            from_rec, from_core = origin(*offsets[j])
            slot = from_rec * cores + from_core
            spread_copy(it, j, slot).wait_recv()
            add_block(slot, False)

        for c in range(chunks):
            rows = pl.ds(c * CHUNK, CHUNK)
            data = jnp.concatenate([shot_sum[rows, :], jnp.zeros((CHUNK, jitter), F32)], axis=1)
            data = pltpu.roll(data, delay, 1)
            up_out[it, rows, :] = data[:, high:].astype(BF)
            down_out[it, rows, :] = data[:, :jitter].astype(BF)
            residual[rows, :] = record[rows, :] - data[:, jitter:high]

            @pl.when(has_after)
            def _():
                up_copy(it, c).start()

            @pl.when(has_before)
            def _():
                down_copy(it, c).start()

        for c in range(chunks):
            rows = pl.ds(c * CHUNK, CHUNK)

            @pl.when(has_before)
            def _():
                up_copy(it, c).wait_recv()
                residual[rows, :] -= up_in[it, rows, :].astype(F32)

            @pl.when(has_after)
            def _():
                down_copy(it, c).wait_recv()
                residual[rows, pl.ds(window - jitter, jitter)] -= down_in[it, rows, :].astype(F32)

            narrow[it, rows, :] = residual[rows, :].astype(BF)

            @pl.when(has_before)
            def _():
                head_copy(it, c).start()

            @pl.when(has_after)
            def _():
                tail_copy(it, c).start()

        for c in range(chunks):
            rows = pl.ds(c * CHUNK, CHUNK)

            @pl.when(has_before)
            def _():
                tail_copy(it, c).wait_recv()

            @pl.when(has_after)
            def _():
                head_copy(it, c).wait_recv()

            data = jnp.concatenate(
                [tail_in[it, rows, :], narrow[it, rows, :], head_in[it, rows, :]], axis=1
            ).astype(F32)
            windows[rows, :] = pltpu.roll(data, back, 1)[:, :time_len].astype(BF)

        if it == 0:
            copy_b.wait()
        for j, (a, b) in enumerate(offsets):
            to_rec, to_core = peer(a, b)
            columns = rows_of(to_rec * cores + to_core, freqs)
            spectra_out[it, j] = dot(windows[...], time_table_t[:, columns]).astype(BF)
            spectra_copy(it, j, me).start()
        spectra_in[it, rows_of(me, traces)] = dot(
            windows[...], time_table_t[:, rows_of(me, freqs)]
        ).astype(BF)

        for a in range(recs):
            for j, (far, _b) in enumerate(offsets):
                if far == a:
                    from_rec, from_core = origin(*offsets[j])
                    spectra_copy(it, j, from_rec * cores + from_core).wait_recv()
            part = rows_of(lax.rem(rec + recs - a, recs), cores * traces)
            last = a == recs - 1

            @pl.loop(0, model.shape[0] // 128)
            def _(i):
                out_rows = pl.ds(pl.multiple_of(i * 128, 128), 128)
                grad = dot(trace_table[out_rows, part], spectra_in[it, part])
                value = model[out_rows, :] + 0.5 * grad
                if last:
                    value = value - jnp.clip(value, -0.3, 0.3)
                    narrow_model[out_rows, :] = value.astype(BF)
                model[out_rows, :] = value

    for it in range(ITERS):
        for j in range(len(offsets)):
            spread_copy(it, j, me).wait_send()
            spectra_copy(it, j, me).wait_send()
        for c in range(chunks):

            @pl.when(has_after)
            def _():
                up_copy(it, c).wait_send()
                tail_copy(it, c).wait_send()

            @pl.when(has_before)
            def _():
                down_copy(it, c).wait_send()
                head_copy(it, c).wait_send()


def shards(model_init, record, activation_dither):
    _, waves, freqs = model_init.shape
    traces, window = record.shape
    recs, cores, shots = lax.axis_size("rec"), lax.axis_size("tr"), lax.axis_size("shot")
    group = recs * cores
    time_len = freqs * group
    jitter = time_len // 4
    time_table, trace_table = cosine_table(time_len), cosine_table(waves)
    chunks = traces // CHUNK
    vmem, hbm = pl.BlockSpec(memory_space=pltpu.VMEM), pl.BlockSpec(memory_space=pl.ANY)
    dma = pltpu.SemaphoreType.DMA
    model, residual = pl.pallas_call(
        functools.partial(kernel, (recs, cores, shots, time_len, freqs, traces, window)),
        out_shape=[
            jax.ShapeDtypeStruct((waves, freqs), F32),
            jax.ShapeDtypeStruct((traces, window), F32),
        ],
        in_specs=[pl.BlockSpec(memory_space=pltpu.SMEM)] + [vmem] * 4 + [hbm] * 2,
        out_specs=[vmem, vmem],
        scratch_shapes=[
            pltpu.VMEM((time_len, time_len), BF),
            pltpu.VMEM((time_len, time_len), BF),
            pltpu.VMEM((waves, freqs), BF),
            pltpu.VMEM((ITERS, group - 1, traces, freqs), BF),
            pltpu.VMEM((ITERS, group, traces, freqs), BF),
            pltpu.VMEM((traces, time_len), F32),
            pltpu.VMEM((ITERS, traces, time_len - window), BF),
            pltpu.VMEM((ITERS, traces, jitter), BF),
            pltpu.VMEM((ITERS, traces, time_len - window), BF),
            pltpu.VMEM((ITERS, traces, jitter), BF),
            pltpu.VMEM((ITERS, traces, window), BF),
            pltpu.VMEM((ITERS, traces, jitter), BF),
            pltpu.VMEM((ITERS, traces, window), BF),
            pltpu.VMEM((traces, time_len), BF),
            pltpu.VMEM((ITERS, group - 1, traces, freqs), BF),
            pltpu.VMEM((ITERS, group * traces, freqs), BF),
            dma((2,)),
            dma((ITERS, group - 1)),
            dma((ITERS, group - 1)),
            dma((ITERS, 2, chunks)),
            dma((ITERS, 2, chunks)),
            dma((ITERS, 2, chunks)),
            dma((ITERS, 2, chunks)),
            dma((ITERS, group - 1)),
            dma((ITERS, group - 1)),
        ],
        compiler_params=pltpu.CompilerParams(
            collective_id=0, has_side_effects=True, vmem_limit_bytes=48 * 1024 * 1024
        ),
        name="deblend",
    )(
        activation_dither, model_init[0], record, jnp.asarray(trace_table),
        jnp.asarray(np.ascontiguousarray(trace_table.T)), jnp.asarray(time_table),
        jnp.asarray(np.ascontiguousarray(time_table.T)),
    )
    return model[None], residual


def solution(mesh):
    return jax.shard_map(
        shards,
        mesh=mesh,
        in_specs=(
            P(("swath", "shot"), None, ("rec", "tr")),
            P(("rec", "tr"), ("swath", "shot")),
            P(("swath", "shot")),
        ),
        out_specs=(P(("swath", "shot"), None, ("rec", "tr")), P(("rec", "tr"), ("swath", "shot"))),
        check_vma=False,
    )
```

```python
import functools
import math

import jax
import jax.numpy as jnp
import ml_dtypes
import numpy as np
from jax import lax
from jax.experimental import pallas as pl
from jax.experimental.pallas import tpu as pltpu
from jax.sharding import PartitionSpec as P

ITERS = 2
PARTS = 2
TILE = 1024
BF = jnp.bfloat16
F32 = jnp.float32


def cosine_table(order):
    column = np.arange(order, dtype=np.int64)
    phase = (2 * column[None, :] + 1) * column[:, None] % (4 * order)
    table = np.cos(np.float32(math.pi) * phase.astype(np.float32) / np.float32(2.0 * order))
    table = table * np.float32(math.sqrt(2.0 / order))
    table = table * np.where(column[:, None] == 0, math.sqrt(0.5), 1.0).astype(np.float32)
    return table.astype(ml_dtypes.bfloat16)


def dot(a, b):
    return jnp.dot(a, b, preferred_element_type=F32)


def kernel(
    sizes, dither, model_hbm, record_hbm, trace_hbm, trace_t_hbm, time_hbm, time_t_hbm,
    model, residual,
    record, trace_table, trace_table_t, time_table, time_table_t, narrow_model, spread_out, spread_in, shot_sum, up_out, down_out,
    up_in, down_in, narrow, tail_in, head_in, windows, spectra_out, spectra_in,
    table_sem, spread_send, spread_recv, part_send, part_recv, res_send, res_recv,
    spectra_send, spectra_recv,
):
    recs, cores, shots, time_len, freqs, traces, window = sizes
    jitter = time_len // 4
    span = time_len + jitter
    high = jitter + window
    rec, core, shot = lax.axis_index("rec"), lax.axis_index("tr"), lax.axis_index("shot")
    me = rec * cores + core
    offsets = [(a, b) for a in range(1, recs) for b in range(cores)]
    offsets += [(0, b) for b in range(1, cores)]
    has_before, has_after = shot > 0, shot < shots - 1

    def peer(a, b):
        return lax.rem(rec + a, recs), lax.rem(core + b, cores)

    def origin(a, b):
        return lax.rem(rec + recs - a, recs), lax.rem(core + cores - b, cores)

    def rows_of(index, size):
        return pl.ds(pl.multiple_of(index * size, size), size)

    loads = [
        pltpu.make_async_copy(source, target, table_sem.at[k])
        for k, (source, target) in enumerate(
            [
                (model_hbm, model), (trace_t_hbm, trace_table_t), (time_hbm, time_table),
                (record_hbm, record), (time_t_hbm, time_table_t), (trace_hbm, trace_table),
            ]
        )
    ]
    for load in loads:
        load.start()

    barrier = pltpu.get_barrier_semaphore()
    for a, b in offsets:
        to_rec, to_core = peer(a, b)
        pl.semaphore_signal(barrier, inc=1, device_id={"rec": to_rec, "tr": to_core})

    @pl.when(has_before)
    def _():
        pl.semaphore_signal(barrier, inc=1, device_id={"shot": shot - 1})

    @pl.when(has_after)
    def _():
        pl.semaphore_signal(barrier, inc=1, device_id={"shot": shot + 1})

    loads[0].wait()
    loads[1].wait()
    narrow_model[...] = model[...].astype(BF)

    @pl.when(jnp.logical_not(has_before))
    def _():
        tail_in[...] = jnp.zeros_like(tail_in)

    @pl.when(jnp.logical_not(has_after))
    def _():
        head_in[...] = jnp.zeros_like(head_in)

    beside = has_before.astype(jnp.int32) + has_after.astype(jnp.int32)
    pl.semaphore_wait(barrier, len(offsets) + beside)

    delay = dither[0]
    back = jnp.where(delay == 0, 0, span - delay)

    half = traces // PARTS
    near = [j for j, (a, _) in enumerate(offsets) if a == 0]
    far = [j for j, (a, _) in enumerate(offsets) if a > 0]

    def parts_of(j):
        return range(1 if j in near else PARTS)

    def part_rows(j, h):
        return (0, traces) if j in near else (h * half, half)

    def spread_copy(it, j, slot, h):
        to_rec, to_core = peer(*offsets[j])
        rows = pl.ds(*part_rows(j, h))
        return pltpu.make_async_remote_copy(
            spread_out.at[it, j, rows], spread_in.at[it, rows, rows_of(slot, freqs)],
            spread_send.at[it, j, h], spread_recv.at[it, j, h],
            device_id={"rec": to_rec, "tr": to_core},
        )

    def spectra_copy(it, j, slot, h):
        to_rec, to_core = peer(*offsets[j])
        first, count = part_rows(j, h)
        place = pl.ds(pl.multiple_of(slot * traces + first, count), count)
        return pltpu.make_async_remote_copy(
            spectra_out.at[it, j, pl.ds(first, count)], spectra_in.at[it, place],
            spectra_send.at[it, j, h], spectra_recv.at[it, j, h],
            device_id={"rec": to_rec, "tr": to_core},
        )

    def up_copy(it, c):
        rows = pl.ds(c * half, half)
        return pltpu.make_async_remote_copy(
            up_out.at[it, rows], up_in.at[it, rows], part_send.at[it, 0, c],
            part_recv.at[it, 0, c], device_id={"shot": shot + 1},
        )

    def down_copy(it, c):
        rows = pl.ds(c * half, half)
        return pltpu.make_async_remote_copy(
            down_out.at[it, rows], down_in.at[it, rows], part_send.at[it, 1, c],
            part_recv.at[it, 1, c], device_id={"shot": shot - 1},
        )

    def tail_copy(it, c):
        rows = pl.ds(c * half, half)
        return pltpu.make_async_remote_copy(
            narrow.at[it, rows, pl.ds(window - jitter, jitter)], tail_in.at[it, rows],
            res_send.at[it, 0, c], res_recv.at[it, 0, c], device_id={"shot": shot + 1},
        )

    def head_copy(it, c):
        rows = pl.ds(c * half, half)
        return pltpu.make_async_remote_copy(
            narrow.at[it, rows], head_in.at[it, rows],
            res_send.at[it, 1, c], res_recv.at[it, 1, c], device_id={"shot": shot - 1},
        )

    for it in range(ITERS):
        for j, (a, b) in enumerate(offsets):
            to_rec, to_core = peer(a, b)
            block = dot(trace_table_t[rows_of(to_rec * cores + to_core, traces), :], narrow_model[...])
            spread_out[it, j] = block.astype(BF)
            spread_copy(it, j, me, 0).start()
        for h in range(1, PARTS):
            for j in far:
                spread_copy(it, j, me, h).start()
        own = dot(trace_table_t[rows_of(me, traces), :], narrow_model[...]).astype(BF)
        spread_in[it, :, rows_of(me, freqs)] = own
        if it == 0:
            loads[2].wait()
            loads[3].wait()

        def add_blocks(from_rec, rows, first):
            depth = rows_of(from_rec, cores * freqs)

            @pl.loop(0, time_len // TILE)
            def _(i):
                columns = pl.ds(pl.multiple_of(i * TILE, TILE), TILE)
                term = dot(spread_in[it, rows, depth], time_table[depth, columns])
                if first:
                    shot_sum[rows, columns] = term
                else:
                    shot_sum[rows, columns] += term

        def await_blocks(js, h):
            for j in js:
                from_rec, from_core = origin(*offsets[j])
                spread_copy(it, j, from_rec * cores + from_core, h).wait_recv()

        await_blocks(near, 0)
        add_blocks(rec, pl.ds(0, traces), True)
        for h in range(PARTS):
            for a in range(1, recs):
                await_blocks([j for j in far if offsets[j][0] == a], h)
                add_blocks(lax.rem(rec + recs - a, recs), pl.ds(h * half, half), False)

            for c in range(h, h + 1):
                rows = pl.ds(c * half, half)
                data = jnp.concatenate([shot_sum[rows, :], jnp.zeros((half, jitter), F32)], axis=1)
                data = pltpu.roll(data, delay, 1)
                up_out[it, rows, :] = data[:, high:].astype(BF)
                down_out[it, rows, :] = data[:, :jitter].astype(BF)
                residual[rows, :] = record[rows, :] - data[:, jitter:high]

                @pl.when(has_after)
                def _():
                    up_copy(it, c).start()

                @pl.when(has_before)
                def _():
                    down_copy(it, c).start()

        for c in range(PARTS):
            rows = pl.ds(c * half, half)

            @pl.when(has_before)
            def _():
                up_copy(it, c).wait_recv()
                residual[rows, :] -= up_in[it, rows, :].astype(F32)

            @pl.when(has_after)
            def _():
                down_copy(it, c).wait_recv()
                residual[rows, pl.ds(window - jitter, jitter)] -= down_in[it, rows, :].astype(F32)

            narrow[it, rows, :] = residual[rows, :].astype(BF)

            @pl.when(has_before)
            def _():
                head_copy(it, c).start()

            @pl.when(has_after)
            def _():
                tail_copy(it, c).start()

        if it == 0:
            loads[4].wait()
            loads[5].wait()
        for h in range(PARTS):
            for c in range(h, h + 1):
                rows = pl.ds(c * half, half)

                @pl.when(has_before)
                def _():
                    tail_copy(it, c).wait_recv()

                @pl.when(has_after)
                def _():
                    head_copy(it, c).wait_recv()

                data = jnp.concatenate(
                    [tail_in[it, rows, :], narrow[it, rows, :], head_in[it, rows, :]], axis=1
                ).astype(F32)
                windows[rows, :] = pltpu.roll(data, back, 1)[:, :time_len].astype(BF)

            rows = pl.ds(h * half, half)
            for j in far:
                to_rec, to_core = peer(*offsets[j])
                columns = rows_of(to_rec * cores + to_core, freqs)
                spectra_out[it, j, rows] = dot(windows[rows, :], time_table_t[:, columns]).astype(BF)
                spectra_copy(it, j, me, h).start()

        for j in near:
            to_rec, to_core = peer(*offsets[j])
            columns = rows_of(to_rec * cores + to_core, freqs)
            spectra_out[it, j] = dot(windows[...], time_table_t[:, columns]).astype(BF)
            spectra_copy(it, j, me, 0).start()
        own = dot(windows[...], time_table_t[:, rows_of(me, freqs)]).astype(BF)
        spectra_in[it, rows_of(me, traces)] = own

        for a in range(recs):
            for j, (away, _) in enumerate(offsets):
                if away == a:
                    from_rec, from_core = origin(*offsets[j])
                    for h in parts_of(j):
                        spectra_copy(it, j, from_rec * cores + from_core, h).wait_recv()
            part = rows_of(lax.rem(rec + recs - a, recs), cores * traces)
            last = a == recs - 1

            @pl.loop(0, model.shape[0] // 128)
            def _(i):
                out_rows = pl.ds(pl.multiple_of(i * 128, 128), 128)
                grad = dot(trace_table[out_rows, part], spectra_in[it, part])
                value = model[out_rows, :] + 0.5 * grad
                if last:
                    value = value - jnp.clip(value, -0.3, 0.3)
                    narrow_model[out_rows, :] = value.astype(BF)
                model[out_rows, :] = value

    for it in range(ITERS):
        for j in range(len(offsets)):
            for h in parts_of(j):
                spread_copy(it, j, me, h).wait_send()
                spectra_copy(it, j, me, h).wait_send()
        for c in range(PARTS):

            @pl.when(has_after)
            def _():
                up_copy(it, c).wait_send()
                tail_copy(it, c).wait_send()

            @pl.when(has_before)
            def _():
                down_copy(it, c).wait_send()
                head_copy(it, c).wait_send()


def shards(model_init, record, activation_dither):
    _, waves, freqs = model_init.shape
    traces, window = record.shape
    recs, cores, shots = lax.axis_size("rec"), lax.axis_size("tr"), lax.axis_size("shot")
    group = recs * cores
    time_len = freqs * group
    jitter = time_len // 4
    time_table, trace_table = cosine_table(time_len), cosine_table(waves)
    vmem, hbm = pl.BlockSpec(memory_space=pltpu.VMEM), pl.BlockSpec(memory_space=pl.ANY)
    dma = pltpu.SemaphoreType.DMA
    model, residual = pl.pallas_call(
        functools.partial(kernel, (recs, cores, shots, time_len, freqs, traces, window)),
        out_shape=[
            jax.ShapeDtypeStruct((waves, freqs), F32),
            jax.ShapeDtypeStruct((traces, window), F32),
        ],
        in_specs=[pl.BlockSpec(memory_space=pltpu.SMEM)] + [hbm] * 6,
        out_specs=[vmem, vmem],
        scratch_shapes=[
            pltpu.VMEM((traces, window), F32),
            pltpu.VMEM((waves, waves), BF),
            pltpu.VMEM((waves, waves), BF),
            pltpu.VMEM((time_len, time_len), BF),
            pltpu.VMEM((time_len, time_len), BF),
            pltpu.VMEM((waves, freqs), BF),
            pltpu.VMEM((ITERS, group - 1, traces, freqs), BF),
            pltpu.VMEM((ITERS, traces, group * freqs), BF),
            pltpu.VMEM((traces, time_len), F32),
            pltpu.VMEM((ITERS, traces, time_len - window), BF),
            pltpu.VMEM((ITERS, traces, jitter), BF),
            pltpu.VMEM((ITERS, traces, time_len - window), BF),
            pltpu.VMEM((ITERS, traces, jitter), BF),
            pltpu.VMEM((ITERS, traces, window), BF),
            pltpu.VMEM((ITERS, traces, jitter), BF),
            pltpu.VMEM((ITERS, traces, window), BF),
            pltpu.VMEM((traces, time_len), BF),
            pltpu.VMEM((ITERS, group - 1, traces, freqs), BF),
            pltpu.VMEM((ITERS, group * traces, freqs), BF),
            dma((6,)),
            dma((ITERS, group - 1, PARTS)),
            dma((ITERS, group - 1, PARTS)),
            dma((ITERS, 2, PARTS)),
            dma((ITERS, 2, PARTS)),
            dma((ITERS, 2, PARTS)),
            dma((ITERS, 2, PARTS)),
            dma((ITERS, group - 1, PARTS)),
            dma((ITERS, group - 1, PARTS)),
        ],
        compiler_params=pltpu.CompilerParams(
            collective_id=0, has_side_effects=True, vmem_limit_bytes=48 * 1024 * 1024
        ),
        name="deblend",
    )(
        activation_dither, model_init[0], record, jnp.asarray(trace_table),
        jnp.asarray(np.ascontiguousarray(trace_table.T)), jnp.asarray(time_table),
        jnp.asarray(np.ascontiguousarray(time_table.T)),
    )
    return model[None], residual


def solution(mesh):
    return jax.shard_map(
        shards,
        mesh=mesh,
        in_specs=(
            P(("swath", "shot"), None, ("rec", "tr")),
            P(("rec", "tr"), ("swath", "shot")),
            P(("swath", "shot")),
        ),
        out_specs=(P(("swath", "shot"), None, ("rec", "tr")), P(("rec", "tr"), ("swath", "shot"))),
        check_vma=False,
    )
```

```python
import functools
import math

import jax
import jax.numpy as jnp
import ml_dtypes
import numpy as np
from jax import lax
from jax.experimental import pallas as pl
from jax.experimental.pallas import tpu as pltpu
from jax.sharding import PartitionSpec as P

ITERS = 2
PARTS = 4
TILE = 1024
BF = jnp.bfloat16
F32 = jnp.float32


def cosine_table(order):
    column = np.arange(order, dtype=np.int64)
    phase = (2 * column[None, :] + 1) * column[:, None] % (4 * order)
    table = np.cos(np.float32(math.pi) * phase.astype(np.float32) / np.float32(2.0 * order))
    table = table * np.float32(math.sqrt(2.0 / order))
    table = table * np.where(column[:, None] == 0, math.sqrt(0.5), 1.0).astype(np.float32)
    return table.astype(ml_dtypes.bfloat16)


def dot(a, b):
    return jnp.dot(a, b, preferred_element_type=F32)


def kernel(
    sizes, dither, model_hbm, record_hbm, trace_hbm, trace_t_hbm, time_hbm, time_t_hbm,
    model, residual,
    record, trace_table, trace_table_t, time_table, time_table_t, narrow_model, spread_out, spread_in, shot_sum, up_out, down_out,
    up_in, down_in, narrow, tail_in, head_in, windows, spectra_out, spectra_in,
    table_sem, spread_send, spread_recv, part_send, part_recv, res_send, res_recv,
    spectra_send, spectra_recv,
):
    recs, cores, shots, time_len, freqs, traces, window = sizes
    jitter = time_len // 4
    span = time_len + jitter
    high = jitter + window
    rec, core, shot = lax.axis_index("rec"), lax.axis_index("tr"), lax.axis_index("shot")
    me = rec * cores + core
    offsets = [(a, b) for a in range(1, recs) for b in range(cores)]
    offsets += [(0, b) for b in range(1, cores)]
    has_before, has_after = shot > 0, shot < shots - 1

    def peer(a, b):
        return lax.rem(rec + a, recs), lax.rem(core + b, cores)

    def origin(a, b):
        return lax.rem(rec + recs - a, recs), lax.rem(core + cores - b, cores)

    def rows_of(index, size):
        return pl.ds(pl.multiple_of(index * size, size), size)

    loads = [
        pltpu.make_async_copy(source, target, table_sem.at[k])
        for k, (source, target) in enumerate(
            [
                (model_hbm, model), (trace_t_hbm, trace_table_t), (time_hbm, time_table),
                (record_hbm, record), (time_t_hbm, time_table_t), (trace_hbm, trace_table),
            ]
        )
    ]
    for load in loads:
        load.start()

    barrier = pltpu.get_barrier_semaphore()
    for a, b in offsets:
        to_rec, to_core = peer(a, b)
        pl.semaphore_signal(barrier, inc=1, device_id={"rec": to_rec, "tr": to_core})

    @pl.when(has_before)
    def _():
        pl.semaphore_signal(barrier, inc=1, device_id={"shot": shot - 1})

    @pl.when(has_after)
    def _():
        pl.semaphore_signal(barrier, inc=1, device_id={"shot": shot + 1})

    loads[0].wait()
    loads[1].wait()
    narrow_model[...] = model[...].astype(BF)

    @pl.when(jnp.logical_not(has_before))
    def _():
        tail_in[...] = jnp.zeros_like(tail_in)

    @pl.when(jnp.logical_not(has_after))
    def _():
        head_in[...] = jnp.zeros_like(head_in)

    beside = has_before.astype(jnp.int32) + has_after.astype(jnp.int32)
    pl.semaphore_wait(barrier, len(offsets) + beside)

    delay = dither[0]
    back = jnp.where(delay == 0, 0, span - delay)

    half = traces // PARTS
    near = [j for j, (a, _) in enumerate(offsets) if a == 0]
    far = [j for j, (a, _) in enumerate(offsets) if a > 0]

    def parts_of(j):
        return range(1 if j in near else PARTS)

    def part_rows(j, h):
        return (0, traces) if j in near else (h * half, half)

    def spread_copy(it, j, slot, h):
        to_rec, to_core = peer(*offsets[j])
        rows = pl.ds(*part_rows(j, h))
        return pltpu.make_async_remote_copy(
            spread_out.at[it, j, rows], spread_in.at[it, rows, rows_of(slot, freqs)],
            spread_send.at[it, j, h], spread_recv.at[it, j, h],
            device_id={"rec": to_rec, "tr": to_core},
        )

    def spectra_copy(it, j, slot, h):
        to_rec, to_core = peer(*offsets[j])
        first, count = part_rows(j, h)
        place = pl.ds(pl.multiple_of(slot * traces + first, count), count)
        return pltpu.make_async_remote_copy(
            spectra_out.at[it, j, pl.ds(first, count)], spectra_in.at[it, place],
            spectra_send.at[it, j, h], spectra_recv.at[it, j, h],
            device_id={"rec": to_rec, "tr": to_core},
        )

    def up_copy(it, c):
        rows = pl.ds(c * half, half)
        return pltpu.make_async_remote_copy(
            up_out.at[it, rows], up_in.at[it, rows], part_send.at[it, 0, c],
            part_recv.at[it, 0, c], device_id={"shot": shot + 1},
        )

    def down_copy(it, c):
        rows = pl.ds(c * half, half)
        return pltpu.make_async_remote_copy(
            down_out.at[it, rows], down_in.at[it, rows], part_send.at[it, 1, c],
            part_recv.at[it, 1, c], device_id={"shot": shot - 1},
        )

    def tail_copy(it, c):
        rows = pl.ds(c * half, half)
        return pltpu.make_async_remote_copy(
            narrow.at[it, rows, pl.ds(window - jitter, jitter)], tail_in.at[it, rows],
            res_send.at[it, 0, c], res_recv.at[it, 0, c], device_id={"shot": shot + 1},
        )

    def head_copy(it, c):
        rows = pl.ds(c * half, half)
        return pltpu.make_async_remote_copy(
            narrow.at[it, rows], head_in.at[it, rows],
            res_send.at[it, 1, c], res_recv.at[it, 1, c], device_id={"shot": shot - 1},
        )

    for it in range(ITERS):
        for j, (a, b) in enumerate(offsets):
            to_rec, to_core = peer(a, b)
            block = dot(trace_table_t[rows_of(to_rec * cores + to_core, traces), :], narrow_model[...])
            spread_out[it, j] = block.astype(BF)
            spread_copy(it, j, me, 0).start()
        for h in range(1, PARTS):
            for j in far:
                spread_copy(it, j, me, h).start()
        own = dot(trace_table_t[rows_of(me, traces), :], narrow_model[...]).astype(BF)
        spread_in[it, :, rows_of(me, freqs)] = own
        if it == 0:
            loads[2].wait()
            loads[3].wait()

        def add_blocks(depth, rows, first):
            @pl.loop(0, time_len // TILE)
            def _(i):
                columns = pl.ds(pl.multiple_of(i * TILE, TILE), TILE)
                term = dot(spread_in[it, rows, depth], time_table[depth, columns])
                if first:
                    shot_sum[rows, columns] = term
                else:
                    shot_sum[rows, columns] += term

        def await_blocks(js, h):
            for j in js:
                from_rec, from_core = origin(*offsets[j])
                spread_copy(it, j, from_rec * cores + from_core, h).wait_recv()

        await_blocks(near, 0)
        add_blocks(rows_of(rec, cores * freqs), pl.ds(0, traces), True)
        for h in range(PARTS):
            for j in far:
                await_blocks([j], h)
                from_rec, from_core = origin(*offsets[j])
                slot = from_rec * cores + from_core
                add_blocks(rows_of(slot, freqs), pl.ds(h * half, half), False)

            for c in range(h, h + 1):
                rows = pl.ds(c * half, half)
                data = jnp.concatenate([shot_sum[rows, :], jnp.zeros((half, jitter), F32)], axis=1)
                data = pltpu.roll(data, delay, 1)
                up_out[it, rows, :] = data[:, high:].astype(BF)
                down_out[it, rows, :] = data[:, :jitter].astype(BF)
                residual[rows, :] = record[rows, :] - data[:, jitter:high]

                @pl.when(has_after)
                def _():
                    up_copy(it, c).start()

                @pl.when(has_before)
                def _():
                    down_copy(it, c).start()

        for c in range(PARTS):
            rows = pl.ds(c * half, half)

            @pl.when(has_before)
            def _():
                up_copy(it, c).wait_recv()
                residual[rows, :] -= up_in[it, rows, :].astype(F32)

            @pl.when(has_after)
            def _():
                down_copy(it, c).wait_recv()
                residual[rows, pl.ds(window - jitter, jitter)] -= down_in[it, rows, :].astype(F32)

            narrow[it, rows, :] = residual[rows, :].astype(BF)

            @pl.when(has_before)
            def _():
                head_copy(it, c).start()

            @pl.when(has_after)
            def _():
                tail_copy(it, c).start()

        if it == 0:
            loads[4].wait()
            loads[5].wait()
        for h in range(PARTS):
            for c in range(h, h + 1):
                rows = pl.ds(c * half, half)

                @pl.when(has_before)
                def _():
                    tail_copy(it, c).wait_recv()

                @pl.when(has_after)
                def _():
                    head_copy(it, c).wait_recv()

                data = jnp.concatenate(
                    [tail_in[it, rows, :], narrow[it, rows, :], head_in[it, rows, :]], axis=1
                ).astype(F32)
                windows[rows, :] = pltpu.roll(data, back, 1)[:, :time_len].astype(BF)

            rows = pl.ds(h * half, half)
            for j in far:
                to_rec, to_core = peer(*offsets[j])
                columns = rows_of(to_rec * cores + to_core, freqs)
                spectra_out[it, j, rows] = dot(windows[rows, :], time_table_t[:, columns]).astype(BF)
                spectra_copy(it, j, me, h).start()

        for j in near:
            to_rec, to_core = peer(*offsets[j])
            columns = rows_of(to_rec * cores + to_core, freqs)
            spectra_out[it, j] = dot(windows[...], time_table_t[:, columns]).astype(BF)
            spectra_copy(it, j, me, 0).start()
        own = dot(windows[...], time_table_t[:, rows_of(me, freqs)]).astype(BF)
        spectra_in[it, rows_of(me, traces)] = own

        for a in range(recs):
            for j, (away, _) in enumerate(offsets):
                if away == a:
                    from_rec, from_core = origin(*offsets[j])
                    for h in parts_of(j):
                        spectra_copy(it, j, from_rec * cores + from_core, h).wait_recv()
            part = rows_of(lax.rem(rec + recs - a, recs), cores * traces)
            last = a == recs - 1

            @pl.loop(0, model.shape[0] // 128)
            def _(i):
                out_rows = pl.ds(pl.multiple_of(i * 128, 128), 128)
                grad = dot(trace_table[out_rows, part], spectra_in[it, part])
                value = model[out_rows, :] + 0.5 * grad
                if last:
                    value = value - jnp.clip(value, -0.3, 0.3)
                    narrow_model[out_rows, :] = value.astype(BF)
                model[out_rows, :] = value

    for it in range(ITERS):
        for j in range(len(offsets)):
            for h in parts_of(j):
                spread_copy(it, j, me, h).wait_send()
                spectra_copy(it, j, me, h).wait_send()
        for c in range(PARTS):

            @pl.when(has_after)
            def _():
                up_copy(it, c).wait_send()
                tail_copy(it, c).wait_send()

            @pl.when(has_before)
            def _():
                down_copy(it, c).wait_send()
                head_copy(it, c).wait_send()


def shards(model_init, record, activation_dither):
    _, waves, freqs = model_init.shape
    traces, window = record.shape
    recs, cores, shots = lax.axis_size("rec"), lax.axis_size("tr"), lax.axis_size("shot")
    group = recs * cores
    time_len = freqs * group
    jitter = time_len // 4
    time_table, trace_table = cosine_table(time_len), cosine_table(waves)
    vmem, hbm = pl.BlockSpec(memory_space=pltpu.VMEM), pl.BlockSpec(memory_space=pl.ANY)
    dma = pltpu.SemaphoreType.DMA
    model, residual = pl.pallas_call(
        functools.partial(kernel, (recs, cores, shots, time_len, freqs, traces, window)),
        out_shape=[
            jax.ShapeDtypeStruct((waves, freqs), F32),
            jax.ShapeDtypeStruct((traces, window), F32),
        ],
        in_specs=[pl.BlockSpec(memory_space=pltpu.SMEM)] + [hbm] * 6,
        out_specs=[vmem, vmem],
        scratch_shapes=[
            pltpu.VMEM((traces, window), F32),
            pltpu.VMEM((waves, waves), BF),
            pltpu.VMEM((waves, waves), BF),
            pltpu.VMEM((time_len, time_len), BF),
            pltpu.VMEM((time_len, time_len), BF),
            pltpu.VMEM((waves, freqs), BF),
            pltpu.VMEM((ITERS, group - 1, traces, freqs), BF),
            pltpu.VMEM((ITERS, traces, group * freqs), BF),
            pltpu.VMEM((traces, time_len), F32),
            pltpu.VMEM((ITERS, traces, time_len - window), BF),
            pltpu.VMEM((ITERS, traces, jitter), BF),
            pltpu.VMEM((ITERS, traces, time_len - window), BF),
            pltpu.VMEM((ITERS, traces, jitter), BF),
            pltpu.VMEM((ITERS, traces, window), BF),
            pltpu.VMEM((ITERS, traces, jitter), BF),
            pltpu.VMEM((ITERS, traces, window), BF),
            pltpu.VMEM((traces, time_len), BF),
            pltpu.VMEM((ITERS, group - 1, traces, freqs), BF),
            pltpu.VMEM((ITERS, group * traces, freqs), BF),
            dma((6,)),
            dma((ITERS, group - 1, PARTS)),
            dma((ITERS, group - 1, PARTS)),
            dma((ITERS, 2, PARTS)),
            dma((ITERS, 2, PARTS)),
            dma((ITERS, 2, PARTS)),
            dma((ITERS, 2, PARTS)),
            dma((ITERS, group - 1, PARTS)),
            dma((ITERS, group - 1, PARTS)),
        ],
        compiler_params=pltpu.CompilerParams(
            collective_id=0, has_side_effects=True, vmem_limit_bytes=48 * 1024 * 1024
        ),
        name="deblend",
    )(
        activation_dither, model_init[0], record, jnp.asarray(trace_table),
        jnp.asarray(np.ascontiguousarray(trace_table.T)), jnp.asarray(time_table),
        jnp.asarray(np.ascontiguousarray(time_table.T)),
    )
    return model[None], residual


def solution(mesh):
    return jax.shard_map(
        shards,
        mesh=mesh,
        in_specs=(
            P(("swath", "shot"), None, ("rec", "tr")),
            P(("rec", "tr"), ("swath", "shot")),
            P(("swath", "shot")),
        ),
        out_specs=(P(("swath", "shot"), None, ("rec", "tr")), P(("rec", "tr"), ("swath", "shot"))),
        check_vma=False,
    )
```
